32 devices in a mesh: tile: 8 (over y, x, core), win: 4 (over z).
Axes of the slice: x: 2, y: 2, z: 4, core: 2. Of those that a mesh axis runs over, the one named last changes fastest.
Arguments:
- signal: bfloat16 [4, 1024, 8192], P('win', 'tile'), may hold values from -6 to 6
- tile_list: int32 [16, 2], P('tile'), may hold values from -1 to 3, as said below
- band_mask: int32 [16, 256, 256], P('tile'), may hold values from 0 to 1, as said below
Outputs:
- stacked: float32 [16, 256, 1024], P('tile', 'win')
The draws below stay inside these ranges and needn't reach their ends.
Inputs may be any that keep to these rules, and one draw needn't show every extreme that they name: `tile_list`: every band tile (row block i, column block j, i <= j <= i + 2, j < 4) stands in exactly one slot; the other slots hold -1 in both entries. Slots are placed at random. `band_mask`: zero on slots holding -1; on a tile it is 1 only where the two channels lie at most 448 apart and both are live.
All inputs are finite; a program needn't handle non-finite values.
Results may differ from the reference program's by a relative error of at most 0.0016.
Values may be sent and summed in bfloat16 or wider, within the bound.
A program may use at most 128 MiB of HBM per device.

```python
import math
import jax
import jax.numpy as jnp
import numpy as np
from jax import lax

CB = 256
NT = 8192
F = 2048
F_LO = 64
LAGS = 4
LAG_STEP = 25
SLOTS = 2
BLOCKS = 4
CHANNELS = 1024
BAND_CH = 448
WINDOWS = 4
N_TILE = 8


def tile_layout(key):
    reach = (BAND_CH + CB - 1) // CB
    listed = []
    for row_block in range(BLOCKS):
        for col_block in range(row_block, min(row_block + reach + 1, BLOCKS)):
            listed.append((row_block, col_block))
    total = N_TILE * SLOTS
    listed = listed + [(-1, -1)] * (total - len(listed))
    table = jnp.asarray(np.array(listed, dtype=np.int32))
    order = jax.random.permutation(jax.random.fold_in(key, 11), total)
    return table[order]


def draw_tile_list(key, part):
    return tile_layout(key).astype(jnp.int32)


def draw_band_mask(key, part):
    layout = tile_layout(key)
    alive = jax.random.randint(jax.random.fold_in(key, 12), (CHANNELS,), 0, 10) > 0
    offsets = jnp.arange(CB).astype(jnp.int32)
    row_chan = jnp.maximum(layout[:, 0:1], 0) * CB + offsets[None, :]
    col_chan = jnp.maximum(layout[:, 1:2], 0) * CB + offsets[None, :]
    valid = layout[:, 0] >= 0
    near = jnp.abs(col_chan[:, None, :] - row_chan[:, :, None]) <= BAND_CH
    live = alive[row_chan][:, :, None] & alive[col_chan][:, None, :]
    return (near & live & valid[:, None, None]).astype(jnp.int32)


def level_of(key, extent, split, least, top_value):
    def one(position, parts):
        steps = jax.random.uniform(jax.random.fold_in(jax.random.fold_in(key, 6), position), (parts,), jnp.float32, least / len(split), top_value / len(split))
        return jnp.repeat(jnp.exp(steps), extent[position] // parts).reshape((-1,) + (1,) * (len(extent) - position - 1))

    factor_of = one(*split[0])
    for cut in split[1:]:
        factor_of = factor_of * one(*cut)
    return factor_of


def noise(own_key, shape, spread, bound, cuts=(), kind=jnp.bfloat16):
    level = level_of(own_key, shape, cuts, -0.22, 0.18) if cuts else 1.0
    drawn = jax.random.normal(own_key, shape, jnp.float32) * spread * level
    return jnp.minimum(jnp.maximum(drawn, -bound), bound).astype(kind)


def setup_inputs(seed: int = 0) -> dict:
    arg_keys = jax.random.split(jax.random.key(seed), 4)
    signal = noise(arg_keys[0], (WINDOWS, CHANNELS, NT), 1.0, 6.0, ((0, 4), (1, 8)))
    tile_list = draw_tile_list(jax.random.fold_in(arg_keys[3], 71), 0)
    band_mask = draw_band_mask(jax.random.fold_in(arg_keys[3], 71), 0)
    return dict(signal=signal, tile_list=tile_list, band_mask=band_mask)


def taper_rows(block):
    values = block.astype(jnp.float32)
    values = values - lax.optimization_barrier(jnp.mean(values, axis=-1, keepdims=True))
    times = jnp.arange(NT).astype(jnp.float32)
    window = 0.5 - 0.5 * jnp.cos(times * (2.0 * math.pi / NT))
    return (values * window).astype(jnp.bfloat16)

def make_basis():
    times = jnp.arange(NT).astype(jnp.int32)
    freqs = (F_LO + jnp.arange(F)).astype(jnp.int32)
    phase = jnp.mod(times[:, None] * freqs[None, :], NT).astype(jnp.float32) * (2.0 * math.pi / NT)
    return jnp.concatenate([jnp.cos(phase), -jnp.sin(phase)], axis=1).astype(jnp.bfloat16)

def whiten(spectrum):
    real_part = spectrum[..., :F]
    imag_part = spectrum[..., F:]
    power = real_part * real_part + imag_part * imag_part
    level = lax.optimization_barrier(jnp.mean(power, axis=-1, keepdims=True))
    scale = 1.0 / jnp.sqrt(power + 0.01 * level + 1e-06)
    return jnp.concatenate([real_part * scale, imag_part * scale], axis=-1).astype(jnp.bfloat16)

def lag_tables():
    lags = (jnp.arange(LAGS) - LAGS // 2).astype(jnp.int32) * LAG_STEP
    freqs = (F_LO + jnp.arange(F)).astype(jnp.int32)
    phase = jnp.mod(lags[:, None] * freqs[None, :], NT).astype(jnp.float32) * (2.0 * math.pi / NT)
    return (jnp.cos(phase), jnp.sin(phase))

def rotate_block(block, cosines, sines):
    values = block.astype(jnp.float32)
    real_part = values[..., :F]
    imag_part = values[..., F:]
    pieces = []
    for k in range(LAGS):
        new_real = real_part * cosines[k] + imag_part * sines[k]
        new_imag = imag_part * cosines[k] - real_part * sines[k]
        pieces.append(jnp.concatenate([new_real, new_imag], axis=-1).astype(jnp.bfloat16))
    return jnp.concatenate(pieces, axis=-2)

def reference(signal, tile_list, band_mask):
    basis = make_basis().astype(jnp.float32)

    def one_window(rows):
        tapered = taper_rows(rows).astype(jnp.float32)
        spectrum = jnp.dot(tapered, basis, preferred_element_type=jnp.float32)
        return whiten(spectrum)
    white = lax.map(one_window, signal)
    cosines, sines = lag_tables()
    norm = 1.0 / math.sqrt(F * WINDOWS)

    def one_slot(entry):
        pair, mask = entry
        row_block = jnp.maximum(pair[0], 0).astype(jnp.int32)
        col_block = jnp.maximum(pair[1], 0).astype(jnp.int32)
        left = lax.dynamic_slice_in_dim(white, row_block * CB, CB, 1)
        right = lax.dynamic_slice_in_dim(white, col_block * CB, CB, 1)
        rotated = rotate_block(right, cosines, sines)
        total = jnp.einsum('wap,wbp->ab', left.astype(jnp.float32), rotated.astype(jnp.float32))
        weights = jnp.tile(mask.astype(jnp.float32), (1, LAGS)) * norm
        return total * weights
    return lax.map(one_slot, (tile_list, band_mask))
```

```python
import math

import jax
import jax.numpy as jnp
import ml_dtypes
import numpy as np
from jax import lax
from jax.sharding import PartitionSpec as P

CB = 256
NT = 8192
F = 2048
F_LO = 64
LAGS = 4
LAG_STEP = 25


def lag_tables():
    lags = (jnp.arange(LAGS) - LAGS // 2) * LAG_STEP
    freqs = F_LO + jnp.arange(F)
    phase = jnp.mod(lags[:, None] * freqs[None, :], NT).astype(jnp.float32) * (2.0 * math.pi / NT)
    return (jnp.cos(phase), jnp.sin(phase))


def rotate_block(block, cosines, sines):
    values = block.astype(jnp.float32)
    real_part = values[:, :F]
    imag_part = values[:, F:]
    pieces = []
    for k in range(LAGS):
        new_real = real_part * cosines[k] + imag_part * sines[k]
        new_imag = imag_part * cosines[k] - real_part * sines[k]
        pieces.append(jnp.concatenate([new_real, new_imag], axis=-1).astype(jnp.bfloat16))
    return jnp.concatenate(pieces, axis=0)


def quarter_table():
    phase = (np.arange(NT // 4)[:, None] * (F_LO + np.arange(F))[None, :]) % NT
    angle = phase * (2.0 * math.pi / NT)
    return np.concatenate([np.cos(angle), np.sin(angle)], axis=1).astype(ml_dtypes.bfloat16)


def transform(rows):
    values = rows.astype(jnp.float32)
    values = values - jnp.mean(values, axis=-1, keepdims=True)
    times = jnp.arange(NT).astype(jnp.float32)
    window = 0.5 - 0.5 * jnp.cos(times * (2.0 * math.pi / NT))
    tapered = (values * window).astype(jnp.bfloat16)
    quarter = NT // 4
    freqs = F_LO + jnp.arange(F)
    table = jnp.asarray(quarter_table())
    real_total = jnp.zeros((rows.shape[0], F), jnp.float32)
    imag_total = jnp.zeros((rows.shape[0], F), jnp.float32)
    for quarter_index in range(4):
        part_rows = tapered[:, quarter_index * quarter : (quarter_index + 1) * quarter]
        product = jnp.dot(part_rows, table, preferred_element_type=jnp.float32)
        cos_part = product[:, :F]
        sin_part = product[:, F:]
        turns = jnp.mod(quarter_index * freqs, 4)[None, :]
        real_add = jnp.where(
            turns == 0,
            cos_part,
            jnp.where(turns == 1, -sin_part, jnp.where(turns == 2, -cos_part, sin_part)),
        )
        imag_add = jnp.where(
            turns == 0,
            -sin_part,
            jnp.where(turns == 1, -cos_part, jnp.where(turns == 2, sin_part, cos_part)),
        )
        real_total = real_total + real_add
        imag_total = imag_total + imag_add
    power = real_total * real_total + imag_total * imag_total
    level = jnp.mean(power, axis=-1, keepdims=True)
    scale = 1.0 / jnp.sqrt(power + 0.01 * level + 1e-06)
    return jnp.concatenate([real_total * scale, imag_total * scale], axis=-1).astype(jnp.bfloat16)


def shards(signal, tile_list, band_mask):
    white = transform(signal[0])
    slot_count = tile_list.shape[0]
    starts = jnp.maximum(tile_list, 0) * CB
    whole = lax.all_gather(white, "tile", axis=0, tiled=True)
    blocks = []
    for slot in range(slot_count):
        left = lax.dynamic_slice_in_dim(whole, starts[slot, 0], CB, 0)
        right = lax.dynamic_slice_in_dim(whole, starts[slot, 1], CB, 0)
        blocks.append((left, right))
    cosines, sines = lag_tables()
    rows_here = CB // lax.axis_size("win")
    norm = 1.0 / math.sqrt(F * lax.axis_size("win"))
    first_row = lax.axis_index("win") * rows_here
    mask_rows = lax.dynamic_slice_in_dim(band_mask, first_row, rows_here, 1)
    weights = jnp.tile(mask_rows.astype(jnp.float32), (1, 1, LAGS)) * norm
    terms = []
    for slot in range(slot_count):
        left, right = blocks[slot]
        rotated = rotate_block(right, cosines, sines)
        terms.append(
            lax.dot_general(
                left, rotated, (((1,), (1,)), ((), ())), preferred_element_type=jnp.float32
            )
        )
    summed = lax.psum_scatter(jnp.stack(terms, axis=0), "win", scatter_dimension=1, tiled=True)
    return summed * weights


def solution(mesh):
    placed = (P("win", "tile", None), P("tile", None), P("tile", None, None))
    return jax.shard_map(
        shards, mesh=mesh, in_specs=placed, out_specs=P("tile", "win", None), check_vma=False
    )
```

```python
import functools
import math

import jax
import jax.numpy as jnp
import ml_dtypes
import numpy as np
from jax import lax
from jax.experimental import pallas as pl
from jax.experimental.pallas import tpu as pltpu
from jax.sharding import PartitionSpec as P

CB = 256
NT = 8192
F = 2048
F_LO = 64
LAGS = 4
LAG_STEP = 25


def quarter_table():
    phase = (np.arange(NT // 4)[:, None] * (F_LO + np.arange(F))[None, :]) % NT
    angle = phase * (2.0 * math.pi / NT)
    return np.concatenate([np.cos(angle), np.sin(angle)], axis=1).astype(ml_dtypes.bfloat16)


def transform(rows):
    values = rows.astype(jnp.float32)
    values = values - jnp.mean(values, axis=-1, keepdims=True)
    times = jnp.arange(NT).astype(jnp.float32)
    window = 0.5 - 0.5 * jnp.cos(times * (2.0 * math.pi / NT))
    tapered = (values * window).astype(jnp.bfloat16)
    quarter = NT // 4
    freqs = F_LO + jnp.arange(F)
    table = jnp.asarray(quarter_table())
    real_total = jnp.zeros((rows.shape[0], F), jnp.float32)
    imag_total = jnp.zeros((rows.shape[0], F), jnp.float32)
    for quarter_index in range(4):
        part_rows = tapered[:, quarter_index * quarter : (quarter_index + 1) * quarter]
        product = jnp.dot(part_rows, table, preferred_element_type=jnp.float32)
        cos_part = product[:, :F]
        sin_part = product[:, F:]
        turns = jnp.mod(quarter_index * freqs, 4)[None, :]
        real_add = jnp.where(
            turns == 0,
            cos_part,
            jnp.where(turns == 1, -sin_part, jnp.where(turns == 2, -cos_part, sin_part)),
        )
        imag_add = jnp.where(
            turns == 0,
            -sin_part,
            jnp.where(turns == 1, -cos_part, jnp.where(turns == 2, sin_part, cos_part)),
        )
        real_total = real_total + real_add
        imag_total = imag_total + imag_add
    power = real_total * real_total + imag_total * imag_total
    level = jnp.mean(power, axis=-1, keepdims=True)
    scale = 1.0 / jnp.sqrt(power + 0.01 * level + 1e-06)
    return jnp.concatenate([real_total * scale, imag_total * scale], axis=-1).astype(jnp.bfloat16)


def lag_tables():
    lags = (np.arange(LAGS) - LAGS // 2) * LAG_STEP
    phase = ((lags[:, None] * (F_LO + np.arange(F))[None, :]) % NT) * (2.0 * math.pi / NT)
    return np.cos(phase).astype(np.float32), np.sin(phase).astype(np.float32)


def correlate_kernel(
    blocks, windows,
    white, pairs, weights, cosines, sines,
    out,
    left, left_next, right_far, rotated, product, outgoing, incoming, own_rows, gathered,
    half_send, half_recv, local_sem, win_send, win_recv, tile_send, tile_recv, pass_send, pass_recv,
):
    half = white.shape[0]
    rows_here = CB // windows
    tile = lax.axis_index("tile")
    win = lax.axis_index("win")
    chip, core = tile // 2, tile % 2
    sibling = chip * 2 + (1 - core)
    my_half = pl.ds(pl.multiple_of(core * half, half), half)

    def holds(which):
        even = which % 2 == 0
        far = which + 2 < blocks
        return [which >= 0, even, far, jnp.logical_and(even, far)]

    mine = holds(chip)
    even, far = mine[1], mine[2]

    def remote(src, dst, send, recv, **where):
        return pltpu.make_async_remote_copy(
            src_ref=src, dst_ref=dst, send_sem=send, recv_sem=recv,
            device_id=where, device_id_type=pl.DeviceIdType.MESH,
        )

    def chip_ahead(step):
        return lax.rem(chip + step, blocks)

    barrier = pltpu.get_barrier_semaphore()
    pl.semaphore_signal(barrier, inc=1, device_id={"tile": sibling}, device_id_type=pl.DeviceIdType.MESH)
    for step in range(1, blocks):
        pl.semaphore_signal(
            barrier, inc=1, device_id={"tile": chip_ahead(step) * 2 + core}, device_id_type=pl.DeviceIdType.MESH
        )
    for step in range(1, windows):
        pl.semaphore_signal(
            barrier, inc=1, device_id={"win": lax.rem(win + step, windows)}, device_id_type=pl.DeviceIdType.MESH
        )
    pl.semaphore_wait(barrier, blocks + windows - 1)

    odd_chip = chip % 2 == 1
    late_chip = chip >= 2
    before = lax.rem(chip + blocks - 1, blocks) * 2 + core
    before2 = lax.rem(chip + blocks - 2, blocks) * 2 + core
    to_before = remote(white, left_next.at[my_half], half_send.at[0], half_recv.at[0], tile=before)
    to_before2 = remote(white, right_far, half_send.at[1], half_recv.at[1], tile=before2)
    to_sibling = remote(white, left.at[my_half], half_send.at[2], half_recv.at[2], tile=sibling)
    pass_on = remote(
        left_next.at[my_half], left_next.at[my_half], half_send.at[3], half_recv.at[3], tile=sibling
    )
    keep = pltpu.make_async_copy(white, left.at[my_half], local_sem)

    pl.when(odd_chip)(to_before.start)
    pl.when(late_chip)(to_before2.start)
    to_sibling.start()
    keep.start()

    def rotate(read):
        width = 512
        for part in range(F // width):
            real_cols = pl.ds(part * width, width)
            imag_cols = pl.ds(F + part * width, width)
            real_part = read(real_cols).astype(jnp.float32)
            imag_part = read(imag_cols).astype(jnp.float32)
            for k in range(LAGS):
                c = cosines[pl.ds(k, 1), real_cols]
                s = sines[pl.ds(k, 1), real_cols]
                lag_rows = pl.ds(k * half, half)
                rotated[lag_rows, real_cols] = (real_part * c + imag_part * s).astype(jnp.bfloat16)
                rotated[lag_rows, imag_cols] = (imag_part * c - real_part * s).astype(jnp.bfloat16)

    def win_copy(t, step):
        peer = lax.rem(win + step, windows)
        rows = pl.ds(pl.multiple_of(peer * rows_here, rows_here), rows_here)
        return remote(
            outgoing.at[t, rows], incoming.at[t, step - 1],
            win_send.at[t, step - 1], win_recv.at[t, step - 1], win=peer,
        )

    def spread(index):
        return 1.0 + index.astype(jnp.float32) / windows

    def multiply(t, rows_ref):
        for part in range(LAGS * half // 256):
            cols = pl.ds(part * 256, 256)
            product[:, cols] = lax.dot_general(
                rows_ref[...], rotated[cols, :], (((1,), (1,)), ((), ())),
                preferred_element_type=jnp.float32,
            )
        outgoing[t] = (product[...] * spread(win)).astype(jnp.bfloat16)
        own_rows[t] = product[pl.ds(pl.multiple_of(win * rows_here, rows_here), rows_here), :]
        for step in range(1, windows):
            win_copy(t, step).start()

    def tile_copy(t, step):
        spot = gathered.at[core, chip, t]
        return remote(
            spot, spot, tile_send.at[t, step - 1], tile_recv.at[t, step - 1], tile=chip_ahead(step) * 2 + core
        )

    def pass_copy(t, step):
        spot = gathered.at[core, chip_ahead(blocks - step), t]
        return remote(spot, spot, pass_send.at[t, step], pass_recv.at[t, step], tile=sibling)

    def collect(t):
        total = own_rows[t]
        for step in range(1, windows):
            win_copy(t, step).wait_recv()
            sender = lax.rem(win + windows - step, windows)
            total = total + incoming[t, step - 1].astype(jnp.float32) / spread(sender)
        gathered[core, chip, t] = total
        for step in range(1, blocks):
            tile_copy(t, step).start()
        pass_copy(t, 0).start()

    keep.wait()
    rotate(lambda cols: white[:, cols])
    to_sibling.wait_recv()
    multiply(0, left)

    @pl.when(even)
    def _():
        to_before.wait_recv()
        pass_on.start()
        rotate(lambda cols: left_next[my_half, cols])
        multiply(1, left)

    collect(0)

    @pl.when(far)
    def _():
        to_before2.wait_recv()
        rotate(lambda cols: right_far[:, cols])
        multiply(2, left)

    @pl.when(even)
    def _():
        pass_on.wait_recv()

    @pl.when(mine[3])
    def _():
        multiply(3, left_next)

    for t in range(1, 4):
        pl.when(mine[t])(functools.partial(collect, t))

    for t in range(4):
        for step in range(1, blocks):

            @pl.when(holds(chip_ahead(blocks - step))[t])
            def _():
                tile_copy(t, step).wait_recv()
                pass_copy(t, step).start()

    for t in range(4):
        for step in range(blocks):

            @pl.when(holds(chip_ahead(blocks - step))[t])
            def _():
                pass_copy(t, step).wait_recv()

    for slot in range(out.shape[0]):
        row_block = pairs[slot, 0]
        distance = pairs[slot, 1] - row_block
        live = row_block >= 0
        row_block = jnp.maximum(row_block, 0)
        step_in = jnp.logical_and(distance == 1, row_block % 2 == 1)
        place = jnp.where(step_in, row_block - 1, row_block)
        which = jnp.where(step_in, 3, distance)
        for side in range(2):
            values = gathered[side, place, which]
            side_cols = pl.ds(side * half, half)
            factor = weights[slot, :, side_cols]
            for k in range(LAGS):
                piece = values[:, k * half : (k + 1) * half] * factor
                out[slot, :, pl.ds(k * CB + side * half, half)] = jnp.where(live, piece, 0.0)

    pl.when(odd_chip)(to_before.wait_send)
    pl.when(late_chip)(to_before2.wait_send)
    to_sibling.wait_send()
    pl.when(even)(pass_on.wait_send)

    for t in range(4):

        @pl.when(mine[t])
        def _():
            for step in range(1, windows):
                win_copy(t, step).wait_send()
            for step in range(1, blocks):
                tile_copy(t, step).wait_send()

        for step in range(blocks):
            pl.when(holds(chip_ahead(blocks - step))[t])(pass_copy(t, step).wait_send)


def shards(signal, tile_list, band_mask):
    white = transform(signal[0])
    slot_count = tile_list.shape[0]
    windows = lax.axis_size("win")
    half = white.shape[0]
    blocks = lax.axis_size("tile") * half // CB
    rows_here = CB // windows
    norm = 1.0 / math.sqrt(F * windows)
    first_row = lax.axis_index("win") * rows_here
    mask_rows = lax.dynamic_slice_in_dim(band_mask, first_row, rows_here, 1)
    weights = mask_rows.astype(jnp.float32) * norm
    cosines, sines = lag_tables()
    vmem = pl.BlockSpec(memory_space=pltpu.VMEM)
    dma = pltpu.SemaphoreType.DMA
    width = LAGS * half
    return pl.pallas_call(
        functools.partial(correlate_kernel, blocks, windows),
        out_shape=jax.ShapeDtypeStruct((slot_count, rows_here, LAGS * CB), jnp.float32),
        in_specs=[vmem, pl.BlockSpec(memory_space=pltpu.SMEM), vmem, vmem, vmem],
        out_specs=vmem,
        scratch_shapes=[
            pltpu.VMEM((CB, 2 * F), jnp.bfloat16),
            pltpu.VMEM((CB, 2 * F), jnp.bfloat16),
            pltpu.VMEM((half, 2 * F), jnp.bfloat16),
            pltpu.VMEM((width, 2 * F), jnp.bfloat16),
            pltpu.VMEM((CB, width), jnp.float32),
            pltpu.VMEM((4, CB, width), jnp.bfloat16),
            pltpu.VMEM((4, windows - 1, rows_here, width), jnp.bfloat16),
            pltpu.VMEM((4, rows_here, width), jnp.float32),
            pltpu.VMEM((2, blocks, 4, rows_here, width), jnp.float32),
            dma((4,)), dma((4,)), dma,
            dma((4, windows - 1)), dma((4, windows - 1)),
            dma((4, blocks - 1)), dma((4, blocks - 1)),
            dma((4, blocks)), dma((4, blocks)),
        ],
        compiler_params=pltpu.CompilerParams(
            collective_id=0, has_side_effects=True, vmem_limit_bytes=48 * 1024 * 1024
        ),
        cost_estimate=pl.CostEstimate(flops=5 * 10**9, bytes_accessed=4 * 10**6, transcendentals=0),
    )(white, tile_list, weights, cosines, sines)


def solution(mesh):
    placed = (P("win", "tile", None), P("tile", None), P("tile", None, None))
    return jax.shard_map(
        shards, mesh=mesh, in_specs=placed, out_specs=P("tile", "win", None), check_vma=False
    )
```

```python
import functools
import math

import jax
import jax.numpy as jnp
import ml_dtypes
import numpy as np
from jax import lax
from jax.experimental import pallas as pl
from jax.experimental.pallas import tpu as pltpu
from jax.sharding import PartitionSpec as P

CB = 256
NT = 8192
F = 2048
F_LO = 64
LAGS = 4
LAG_STEP = 25


BINS = 256
ORDER = np.argsort((F_LO + np.arange(F)) % 4, kind="stable")
FREQS = F_LO + ORDER


def quarter_table():
    phase = (np.arange(NT // 4)[:, None] * FREQS[None, :]) % NT
    angle = (phase * (2.0 * math.pi / NT)).reshape(NT // 4, F // BINS, 1, BINS)
    both = np.concatenate([np.cos(angle), np.sin(angle)], axis=2)
    return both.transpose(1, 0, 2, 3).reshape(F // BINS, NT // 4, 2 * BINS).astype(ml_dtypes.bfloat16)


def lag_tables():
    lags = (np.arange(LAGS) - LAGS // 2) * LAG_STEP
    phase = ((lags[:, None] * FREQS[None, :]) % NT) * (2.0 * math.pi / NT)
    return np.cos(phase).astype(np.float32), np.sin(phase).astype(np.float32)


def transform_kernel(signal, window, table, white, tapered, spectrum, power_sum):
    rows = signal.shape[1]
    quarter = NT // 4
    step = pl.program_id(0)

    @pl.when(step == 0)
    def _():
        total = jnp.zeros((rows, 1), jnp.float32)
        for part in range(4):
            values = signal[0, :, part * quarter : (part + 1) * quarter].astype(jnp.float32)
            total = total + jnp.sum(values, axis=-1, keepdims=True)
        mean = total / NT
        for part in range(4):
            cols = pl.ds(part * quarter, quarter)
            values = (signal[0, :, cols].astype(jnp.float32) - mean) * window[:, cols]
            tapered[pl.ds(part * rows, rows), :] = values.astype(jnp.bfloat16)
        power_sum[...] = jnp.zeros_like(power_sum)

    product = jnp.dot(tapered[...], table[0], preferred_element_type=jnp.float32)
    residue = step // (F // 4 // BINS)
    real_total = product[:rows, :BINS]
    imag_total = -product[:rows, BINS:]
    for part in range(1, 4):
        cos_part = product[part * rows : (part + 1) * rows, :BINS]
        sin_part = product[part * rows : (part + 1) * rows, BINS:]
        turn = (part * residue) % 4
        c = jnp.where(turn == 0, 1.0, jnp.where(turn == 2, -1.0, 0.0))
        d = jnp.where(turn == 1, -1.0, jnp.where(turn == 3, 1.0, 0.0))
        real_total = real_total + (c * cos_part + d * sin_part)
        imag_total = imag_total + (d * cos_part - c * sin_part)
    start = pl.multiple_of(step * BINS, BINS)
    spectrum[:, pl.ds(start, BINS)] = real_total
    spectrum[:, pl.ds(F + start, BINS)] = imag_total
    power = real_total * real_total + imag_total * imag_total
    power_sum[...] += jnp.sum(power, axis=-1, keepdims=True)

    @pl.when(step == F // BINS - 1)
    def _():
        floor = 0.01 * (power_sum[...] / F) + 1e-06
        for part in range(F // 512):
            real_cols = pl.ds(part * 512, 512)
            imag_cols = pl.ds(F + part * 512, 512)
            real_part = spectrum[:, real_cols]
            imag_part = spectrum[:, imag_cols]
            scale = lax.rsqrt(real_part * real_part + imag_part * imag_part + floor)
            white[:, real_cols] = (real_part * scale).astype(jnp.bfloat16)
            white[:, imag_cols] = (imag_part * scale).astype(jnp.bfloat16)


def transform(signal):
    rows = signal.shape[1]
    window = (0.5 - 0.5 * np.cos(np.arange(NT) * (2.0 * math.pi / NT))).astype(np.float32)[None]
    return pl.pallas_call(
        transform_kernel,
        grid=(F // BINS,),
        out_shape=jax.ShapeDtypeStruct((rows, 2 * F), jnp.bfloat16),
        in_specs=[
            pl.BlockSpec((1, rows, NT), lambda step: (0, 0, 0)),
            pl.BlockSpec((1, NT), lambda step: (0, 0)),
            pl.BlockSpec((1, NT // 4, 2 * BINS), lambda step: (step, 0, 0)),
        ],
        out_specs=pl.BlockSpec((rows, 2 * F), lambda step: (0, 0)),
        scratch_shapes=[
            pltpu.VMEM((4 * rows, NT // 4), jnp.bfloat16),
            pltpu.VMEM((rows, 2 * F), jnp.float32),
            pltpu.VMEM((rows, 1), jnp.float32),
        ],
        compiler_params=pltpu.CompilerParams(vmem_limit_bytes=40 * 1024 * 1024),
        cost_estimate=pl.CostEstimate(flops=9 * 10**9, bytes_accessed=20 * 10**6, transcendentals=0),
    )(signal, window, quarter_table())


def correlate_kernel(
    blocks, windows,
    white, pairs, weights, cosines, sines,
    out,
    left, left_next, right_far, rotated, product, outgoing, incoming, own_rows, gathered,
    half_send, half_recv, local_sem, win_send, win_recv, tile_send, tile_recv, pass_send, pass_recv,
):
    half = white.shape[0]
    rows_here = CB // windows
    tile = lax.axis_index("tile")
    win = lax.axis_index("win")
    chip, core = tile // 2, tile % 2
    sibling = chip * 2 + (1 - core)
    my_half = pl.ds(pl.multiple_of(core * half, half), half)

    def holds(which):
        even = which % 2 == 0
        far = which + 2 < blocks
        return [which >= 0, even, far, jnp.logical_and(even, far)]

    mine = holds(chip)
    even, far = mine[1], mine[2]

    def remote(src, dst, send, recv, **where):
        return pltpu.make_async_remote_copy(
            src_ref=src, dst_ref=dst, send_sem=send, recv_sem=recv,
            device_id=where, device_id_type=pl.DeviceIdType.MESH,
        )

    def chip_ahead(step):
        return lax.rem(chip + step, blocks)

    barrier = pltpu.get_barrier_semaphore()
    pl.semaphore_signal(barrier, inc=1, device_id={"tile": sibling}, device_id_type=pl.DeviceIdType.MESH)
    for step in range(1, blocks):
        pl.semaphore_signal(
            barrier, inc=1, device_id={"tile": chip_ahead(step) * 2 + core}, device_id_type=pl.DeviceIdType.MESH
        )
    for step in range(1, windows):
        pl.semaphore_signal(
            barrier, inc=1, device_id={"win": lax.rem(win + step, windows)}, device_id_type=pl.DeviceIdType.MESH
        )
    pl.semaphore_wait(barrier, blocks + windows - 1)

    odd_chip = chip % 2 == 1
    late_chip = chip >= 2
    before = lax.rem(chip + blocks - 1, blocks) * 2 + core
    before2 = lax.rem(chip + blocks - 2, blocks) * 2 + core
    to_before = remote(white, left_next.at[my_half], half_send.at[0], half_recv.at[0], tile=before)
    to_before2 = remote(white, right_far, half_send.at[1], half_recv.at[1], tile=before2)
    to_sibling = remote(white, left.at[my_half], half_send.at[2], half_recv.at[2], tile=sibling)
    pass_on = remote(
        left_next.at[my_half], left_next.at[my_half], half_send.at[3], half_recv.at[3], tile=sibling
    )
    keep = pltpu.make_async_copy(white, left.at[my_half], local_sem)

    pl.when(odd_chip)(to_before.start)
    pl.when(late_chip)(to_before2.start)
    to_sibling.start()
    keep.start()

    def rotate(read):
        width = 512
        for part in range(F // width):
            real_cols = pl.ds(part * width, width)
            imag_cols = pl.ds(F + part * width, width)
            real_part = read(real_cols).astype(jnp.float32)
            imag_part = read(imag_cols).astype(jnp.float32)
            for k in range(LAGS):
                c = cosines[pl.ds(k, 1), real_cols]
                s = sines[pl.ds(k, 1), real_cols]
                lag_rows = pl.ds(k * half, half)
                rotated[lag_rows, real_cols] = (real_part * c + imag_part * s).astype(jnp.bfloat16)
                rotated[lag_rows, imag_cols] = (imag_part * c - real_part * s).astype(jnp.bfloat16)

    def win_copy(t, step):
        peer = lax.rem(win + step, windows)
        rows = pl.ds(pl.multiple_of(peer * rows_here, rows_here), rows_here)
        return remote(
            outgoing.at[t, rows], incoming.at[t, step - 1],
            win_send.at[t, step - 1], win_recv.at[t, step - 1], win=peer,
        )

    def spread(index):
        return 1.0 + index.astype(jnp.float32) / windows

    def multiply(t, rows_ref):
        for part in range(LAGS * half // 256):
            cols = pl.ds(part * 256, 256)
            product[:, cols] = lax.dot_general(
                rows_ref[...], rotated[cols, :], (((1,), (1,)), ((), ())),
                preferred_element_type=jnp.float32,
            )
        outgoing[t] = (product[...] * spread(win)).astype(jnp.bfloat16)
        own_rows[t] = product[pl.ds(pl.multiple_of(win * rows_here, rows_here), rows_here), :]
        for step in range(1, windows):
            win_copy(t, step).start()

    def tile_copy(t, step):
        spot = gathered.at[core, chip, t]
        return remote(
            spot, spot, tile_send.at[t, step - 1], tile_recv.at[t, step - 1], tile=chip_ahead(step) * 2 + core
        )

    def pass_copy(t, step):
        spot = gathered.at[core, chip_ahead(blocks - step), t]
        return remote(spot, spot, pass_send.at[t, step], pass_recv.at[t, step], tile=sibling)

    def collect(t):
        total = own_rows[t]
        for step in range(1, windows):
            win_copy(t, step).wait_recv()
            sender = lax.rem(win + windows - step, windows)
            total = total + incoming[t, step - 1].astype(jnp.float32) / spread(sender)
        gathered[core, chip, t] = total
        for step in range(1, blocks):
            tile_copy(t, step).start()
        pass_copy(t, 0).start()

    keep.wait()
    rotate(lambda cols: white[:, cols])
    to_sibling.wait_recv()
    multiply(0, left)

    @pl.when(even)
    def _():
        to_before.wait_recv()
        pass_on.start()
        rotate(lambda cols: left_next[my_half, cols])
        multiply(1, left)

    collect(0)

    @pl.when(far)
    def _():
        to_before2.wait_recv()
        rotate(lambda cols: right_far[:, cols])
        multiply(2, left)

    @pl.when(even)
    def _():
        pass_on.wait_recv()

    @pl.when(mine[3])
    def _():
        multiply(3, left_next)

    for t in range(1, 4):
        pl.when(mine[t])(functools.partial(collect, t))

    for t in range(4):
        for step in range(1, blocks):

            @pl.when(holds(chip_ahead(blocks - step))[t])
            def _():
                tile_copy(t, step).wait_recv()
                pass_copy(t, step).start()

    for t in range(4):
        for step in range(blocks):

            @pl.when(holds(chip_ahead(blocks - step))[t])
            def _():
                pass_copy(t, step).wait_recv()

    for slot in range(out.shape[0]):
        row_block = pairs[slot, 0]
        distance = pairs[slot, 1] - row_block
        live = row_block >= 0
        row_block = jnp.maximum(row_block, 0)
        step_in = jnp.logical_and(distance == 1, row_block % 2 == 1)
        place = jnp.where(step_in, row_block - 1, row_block)
        which = jnp.where(step_in, 3, distance)
        for side in range(2):
            values = gathered[side, place, which]
            side_cols = pl.ds(side * half, half)
            factor = weights[slot, :, side_cols]
            for k in range(LAGS):
                piece = values[:, k * half : (k + 1) * half] * factor
                out[slot, :, pl.ds(k * CB + side * half, half)] = jnp.where(live, piece, 0.0)

    pl.when(odd_chip)(to_before.wait_send)
    pl.when(late_chip)(to_before2.wait_send)
    to_sibling.wait_send()
    pl.when(even)(pass_on.wait_send)

    for t in range(4):

        @pl.when(mine[t])
        def _():
            for step in range(1, windows):
                win_copy(t, step).wait_send()
            for step in range(1, blocks):
                tile_copy(t, step).wait_send()

        for step in range(blocks):
            pl.when(holds(chip_ahead(blocks - step))[t])(pass_copy(t, step).wait_send)


def shards(signal, tile_list, band_mask):
    white = transform(signal)
    slot_count = tile_list.shape[0]
    windows = lax.axis_size("win")
    half = white.shape[0]
    blocks = lax.axis_size("tile") * half // CB
    rows_here = CB // windows
    norm = 1.0 / math.sqrt(F * windows)
    first_row = lax.axis_index("win") * rows_here
    mask_rows = lax.dynamic_slice_in_dim(band_mask, first_row, rows_here, 1)
    weights = mask_rows.astype(jnp.float32) * norm
    cosines, sines = lag_tables()
    vmem = pl.BlockSpec(memory_space=pltpu.VMEM)
    dma = pltpu.SemaphoreType.DMA
    width = LAGS * half
    return pl.pallas_call(
        functools.partial(correlate_kernel, blocks, windows),
        out_shape=jax.ShapeDtypeStruct((slot_count, rows_here, LAGS * CB), jnp.float32),
        in_specs=[vmem, pl.BlockSpec(memory_space=pltpu.SMEM), vmem, vmem, vmem],
        out_specs=vmem,
        scratch_shapes=[
            pltpu.VMEM((CB, 2 * F), jnp.bfloat16),
            pltpu.VMEM((CB, 2 * F), jnp.bfloat16),
            pltpu.VMEM((half, 2 * F), jnp.bfloat16),
            pltpu.VMEM((width, 2 * F), jnp.bfloat16),
            pltpu.VMEM((CB, width), jnp.float32),
            pltpu.VMEM((4, CB, width), jnp.bfloat16),
            pltpu.VMEM((4, windows - 1, rows_here, width), jnp.bfloat16),
            pltpu.VMEM((4, rows_here, width), jnp.float32),
            pltpu.VMEM((2, blocks, 4, rows_here, width), jnp.float32),
            dma((4,)), dma((4,)), dma,
            dma((4, windows - 1)), dma((4, windows - 1)),
            dma((4, blocks - 1)), dma((4, blocks - 1)),
            dma((4, blocks)), dma((4, blocks)),
        ],
        compiler_params=pltpu.CompilerParams(
            collective_id=0, has_side_effects=True, vmem_limit_bytes=48 * 1024 * 1024
        ),
        cost_estimate=pl.CostEstimate(flops=5 * 10**9, bytes_accessed=4 * 10**6, transcendentals=0),
    )(white, tile_list, weights, cosines, sines)


def solution(mesh):
    placed = (P("win", "tile", None), P("tile", None), P("tile", None, None))
    return jax.shard_map(
        shards, mesh=mesh, in_specs=placed, out_specs=P("tile", "win", None), check_vma=False
    )
```

```python
import functools
import math

import jax
import jax.numpy as jnp
import ml_dtypes
import numpy as np
from jax import lax
from jax.experimental import pallas as pl
from jax.experimental.pallas import tpu as pltpu
from jax.sharding import PartitionSpec as P

CB = 256
NT = 8192
F = 2048
F_LO = 64
LAGS = 4
LAG_STEP = 25


BINS = 256
ORDER = np.argsort((F_LO + np.arange(F)) % 4, kind="stable")
FREQS = F_LO + ORDER


def quarter_table():
    phase = (np.arange(NT // 4)[:, None] * FREQS[None, :]) % NT
    angle = (phase * (2.0 * math.pi / NT)).reshape(NT // 4, F // BINS, 1, BINS)
    both = np.concatenate([np.cos(angle), np.sin(angle)], axis=2)
    return both.transpose(1, 0, 2, 3).reshape(F // BINS, NT // 4, 2 * BINS).astype(ml_dtypes.bfloat16)


def lag_tables():
    lags = (np.arange(LAGS) - LAGS // 2) * LAG_STEP
    phase = ((lags[:, None] * FREQS[None, :]) % NT) * (2.0 * math.pi / NT)
    return np.cos(phase).astype(np.float32), np.sin(phase).astype(np.float32)


def transform_kernel(signal, window, table, white, tapered, spectrum, power_sum):
    rows = signal.shape[1]
    quarter = NT // 4
    step = pl.program_id(0)

    @pl.when(step == 0)
    def _():
        total = jnp.zeros((rows, 1), jnp.float32)
        for part in range(4):
            values = signal[0, :, part * quarter : (part + 1) * quarter].astype(jnp.float32)
            total = total + jnp.sum(values, axis=-1, keepdims=True)
        mean = total / NT
        for part in range(4):
            cols = pl.ds(part * quarter, quarter)
            values = (signal[0, :, cols].astype(jnp.float32) - mean) * window[:, cols]
            tapered[pl.ds(part * rows, rows), :] = values.astype(jnp.bfloat16)
        power_sum[...] = jnp.zeros_like(power_sum)

    product = jnp.dot(tapered[...], table[0], preferred_element_type=jnp.float32)
    residue = step // (F // 4 // BINS)
    real_total = product[:rows, :BINS]
    imag_total = -product[:rows, BINS:]
    for part in range(1, 4):
        cos_part = product[part * rows : (part + 1) * rows, :BINS]
        sin_part = product[part * rows : (part + 1) * rows, BINS:]
        turn = (part * residue) % 4
        c = jnp.where(turn == 0, 1.0, jnp.where(turn == 2, -1.0, 0.0))
        d = jnp.where(turn == 1, -1.0, jnp.where(turn == 3, 1.0, 0.0))
        real_total = real_total + (c * cos_part + d * sin_part)
        imag_total = imag_total + (d * cos_part - c * sin_part)
    start = pl.multiple_of(step * BINS, BINS)
    spectrum[:, pl.ds(start, BINS)] = real_total
    spectrum[:, pl.ds(F + start, BINS)] = imag_total
    power = real_total * real_total + imag_total * imag_total
    power_sum[...] += jnp.sum(power, axis=-1, keepdims=True)

    @pl.when(step == F // BINS - 1)
    def _():
        floor = 0.01 * (power_sum[...] / F) + 1e-06
        for part in range(F // 512):
            real_cols = pl.ds(part * 512, 512)
            imag_cols = pl.ds(F + part * 512, 512)
            real_part = spectrum[:, real_cols]
            imag_part = spectrum[:, imag_cols]
            scale = lax.rsqrt(real_part * real_part + imag_part * imag_part + floor)
            white[:, real_cols] = (real_part * scale).astype(jnp.bfloat16)
            white[:, imag_cols] = (imag_part * scale).astype(jnp.bfloat16)


def transform(signal):
    rows = signal.shape[1]
    window = (0.5 - 0.5 * np.cos(np.arange(NT) * (2.0 * math.pi / NT))).astype(np.float32)[None]
    return pl.pallas_call(
        transform_kernel,
        grid=(F // BINS,),
        out_shape=jax.ShapeDtypeStruct((rows, 2 * F), jnp.bfloat16),
        in_specs=[
            pl.BlockSpec((1, rows, NT), lambda step: (0, 0, 0)),
            pl.BlockSpec((1, NT), lambda step: (0, 0)),
            pl.BlockSpec((1, NT // 4, 2 * BINS), lambda step: (step, 0, 0)),
        ],
        out_specs=pl.BlockSpec((rows, 2 * F), lambda step: (0, 0)),
        scratch_shapes=[
            pltpu.VMEM((4 * rows, NT // 4), jnp.bfloat16),
            pltpu.VMEM((rows, 2 * F), jnp.float32),
            pltpu.VMEM((rows, 1), jnp.float32),
        ],
        compiler_params=pltpu.CompilerParams(vmem_limit_bytes=56 * 1024 * 1024),
        cost_estimate=pl.CostEstimate(flops=9 * 10**9, bytes_accessed=20 * 10**6, transcendentals=0),
    )(signal, window, quarter_table())


def correlate_kernel(
    blocks, windows,
    white, pairs, weights, cosines, sines,
    out,
    left, left_next, right_near, right_far, rotated, product, outgoing, incoming, own_rows, gathered,
    half_send, half_recv, local_sem, win_send, win_recv, tile_send, tile_recv, pass_send, pass_recv,
):
    half = white.shape[0]
    rows_here = CB // windows
    tile = lax.axis_index("tile")
    win = lax.axis_index("win")
    chip, core = tile // 2, tile % 2
    sibling = chip * 2 + (1 - core)
    my_half = pl.ds(pl.multiple_of(core * half, half), half)

    def holds(which):
        even = which % 2 == 0
        far = which + 2 < blocks
        across = jnp.logical_and(which % 2 == 1, which >= 3)
        return [which >= 0, even, far, across]

    mine = holds(chip)
    even, far, across = mine[1], mine[2], mine[3]

    def remote(src, dst, send, recv, **where):
        return pltpu.make_async_remote_copy(
            src_ref=src, dst_ref=dst, send_sem=send, recv_sem=recv,
            device_id=where, device_id_type=pl.DeviceIdType.MESH,
        )

    def chip_ahead(step):
        return lax.rem(chip + step, blocks)

    barrier = pltpu.get_barrier_semaphore()
    pl.semaphore_signal(barrier, inc=1, device_id={"tile": sibling}, device_id_type=pl.DeviceIdType.MESH)
    for step in range(1, blocks):
        pl.semaphore_signal(
            barrier, inc=1, device_id={"tile": chip_ahead(step) * 2 + core}, device_id_type=pl.DeviceIdType.MESH
        )
    for step in range(1, windows):
        pl.semaphore_signal(
            barrier, inc=1, device_id={"win": lax.rem(win + step, windows)}, device_id_type=pl.DeviceIdType.MESH
        )
    pl.semaphore_wait(barrier, blocks + windows - 1)

    sends_near = chip >= 1
    sends_far = chip >= 2
    sends_left = jnp.logical_and(chip % 2 == 1, far)
    partner = lax.rem(chip + 1 - 2 * (chip % 2) + blocks, blocks) * 2 + core
    to_near = remote(white, right_near, half_send.at[0], half_recv.at[0], tile=partner)
    to_far = remote(white, right_far, half_send.at[1], half_recv.at[1], tile=chip_ahead(blocks - 2) * 2 + core)
    to_left = remote(
        white, left_next.at[my_half], half_send.at[4], half_recv.at[4], tile=chip_ahead(2) * 2 + core
    )
    to_sibling = remote(white, left.at[my_half], half_send.at[2], half_recv.at[2], tile=sibling)
    pass_on = remote(
        left_next.at[my_half], left_next.at[my_half], half_send.at[3], half_recv.at[3], tile=sibling
    )
    keep = pltpu.make_async_copy(white, left.at[my_half], local_sem)

    pl.when(sends_near)(to_near.start)
    pl.when(sends_far)(to_far.start)
    pl.when(sends_left)(to_left.start)
    to_sibling.start()
    keep.start()

    def rotate(read):
        width = 512
        for part in range(F // width):
            real_cols = pl.ds(part * width, width)
            imag_cols = pl.ds(F + part * width, width)
            real_part = read(real_cols).astype(jnp.float32)
            imag_part = read(imag_cols).astype(jnp.float32)
            for k in range(LAGS):
                c = cosines[pl.ds(k, 1), real_cols]
                s = sines[pl.ds(k, 1), real_cols]
                lag_rows = pl.ds(k * half, half)
                rotated[lag_rows, real_cols] = (real_part * c + imag_part * s).astype(jnp.bfloat16)
                rotated[lag_rows, imag_cols] = (imag_part * c - real_part * s).astype(jnp.bfloat16)

    def win_copy(t, step):
        peer = lax.rem(win + step, windows)
        rows = pl.ds(pl.multiple_of(peer * rows_here, rows_here), rows_here)
        return remote(
            outgoing.at[t, rows], incoming.at[t, step - 1],
            win_send.at[t, step - 1], win_recv.at[t, step - 1], win=peer,
        )

    def spread(index):
        return 1.0 + index.astype(jnp.float32) / windows

    def multiply(t, rows_ref):
        for part in range(LAGS * half // 256):
            cols = pl.ds(part * 256, 256)
            product[:, cols] = lax.dot_general(
                rows_ref[...], rotated[cols, :], (((1,), (1,)), ((), ())),
                preferred_element_type=jnp.float32,
            )
        outgoing[t] = (product[...] * spread(win)).astype(jnp.bfloat16)
        own_rows[t] = product[pl.ds(pl.multiple_of(win * rows_here, rows_here), rows_here), :]
        for step in range(1, windows):
            win_copy(t, step).start()

    def tile_copy(t, step):
        spot = gathered.at[core, chip, t]
        return remote(
            spot, spot, tile_send.at[t, step - 1], tile_recv.at[t, step - 1], tile=chip_ahead(step) * 2 + core
        )

    def pass_copy(t, step):
        spot = gathered.at[core, chip_ahead(blocks - step), t]
        return remote(spot, spot, pass_send.at[t, step], pass_recv.at[t, step], tile=sibling)

    def collect(t):
        total = own_rows[t]
        for step in range(1, windows):
            win_copy(t, step).wait_recv()
            sender = lax.rem(win + windows - step, windows)
            total = total + incoming[t, step - 1].astype(jnp.float32) / spread(sender)
        gathered[core, chip, t] = total
        for step in range(1, blocks):
            tile_copy(t, step).start()
        pass_copy(t, 0).start()

    keep.wait()
    rotate(lambda cols: white[:, cols])
    to_sibling.wait_recv()
    multiply(0, left)

    collect(0)

    @pl.when(even)
    def _():
        to_near.wait_recv()
        rotate(lambda cols: right_near[:, cols])
        multiply(1, left)

    @pl.when(far)
    def _():
        to_far.wait_recv()
        rotate(lambda cols: right_far[:, cols])
        multiply(2, left)

    @pl.when(across)
    def _():
        to_left.wait_recv()
        pass_on.start()
        to_near.wait_recv()
        rotate(lambda cols: right_near[:, cols])
        pass_on.wait_recv()
        multiply(3, left_next)

    for t in range(1, 4):
        pl.when(mine[t])(functools.partial(collect, t))

    for t in range(4):
        for step in range(1, blocks):

            @pl.when(holds(chip_ahead(blocks - step))[t])
            def _():
                tile_copy(t, step).wait_recv()
                pass_copy(t, step).start()

    for t in range(4):
        for step in range(blocks):

            @pl.when(holds(chip_ahead(blocks - step))[t])
            def _():
                pass_copy(t, step).wait_recv()

    for slot in range(out.shape[0]):
        row_block = pairs[slot, 0]
        distance = pairs[slot, 1] - row_block
        live = row_block >= 0
        row_block = jnp.maximum(row_block, 0)
        step_in = jnp.logical_and(distance == 1, row_block % 2 == 1)
        place = jnp.where(step_in, row_block + 2, row_block)
        which = jnp.where(step_in, 3, distance)
        for side in range(2):
            values = gathered[side, place, which]
            side_cols = pl.ds(side * half, half)
            factor = weights[slot, :, side_cols]
            for k in range(LAGS):
                piece = values[:, k * half : (k + 1) * half] * factor
                out[slot, :, pl.ds(k * CB + side * half, half)] = jnp.where(live, piece, 0.0)

    pl.when(sends_near)(to_near.wait_send)
    pl.when(sends_far)(to_far.wait_send)
    pl.when(sends_left)(to_left.wait_send)
    to_sibling.wait_send()
    pl.when(across)(pass_on.wait_send)

    for t in range(4):

        @pl.when(mine[t])
        def _():
            for step in range(1, windows):
                win_copy(t, step).wait_send()
            for step in range(1, blocks):
                tile_copy(t, step).wait_send()

        for step in range(blocks):
            pl.when(holds(chip_ahead(blocks - step))[t])(pass_copy(t, step).wait_send)


def shards(signal, tile_list, band_mask):
    white = transform(signal)
    slot_count = tile_list.shape[0]
    windows = lax.axis_size("win")
    half = white.shape[0]
    blocks = lax.axis_size("tile") * half // CB
    rows_here = CB // windows
    norm = 1.0 / math.sqrt(F * windows)
    first_row = lax.axis_index("win") * rows_here
    mask_rows = lax.dynamic_slice_in_dim(band_mask, first_row, rows_here, 1)
    weights = mask_rows.astype(jnp.float32) * norm
    cosines, sines = lag_tables()
    vmem = pl.BlockSpec(memory_space=pltpu.VMEM)
    dma = pltpu.SemaphoreType.DMA
    width = LAGS * half
    return pl.pallas_call(
        functools.partial(correlate_kernel, blocks, windows),
        out_shape=jax.ShapeDtypeStruct((slot_count, rows_here, LAGS * CB), jnp.float32),
        in_specs=[vmem, pl.BlockSpec(memory_space=pltpu.SMEM), vmem, vmem, vmem],
        out_specs=vmem,
        scratch_shapes=[
            pltpu.VMEM((CB, 2 * F), jnp.bfloat16),
            pltpu.VMEM((CB, 2 * F), jnp.bfloat16),
            pltpu.VMEM((half, 2 * F), jnp.bfloat16),
            pltpu.VMEM((half, 2 * F), jnp.bfloat16),
            pltpu.VMEM((width, 2 * F), jnp.bfloat16),
            pltpu.VMEM((CB, width), jnp.float32),
            pltpu.VMEM((4, CB, width), jnp.bfloat16),
            pltpu.VMEM((4, windows - 1, rows_here, width), jnp.bfloat16),
            pltpu.VMEM((4, rows_here, width), jnp.float32),
            pltpu.VMEM((2, blocks, 4, rows_here, width), jnp.float32),
            dma((5,)), dma((5,)), dma,
            dma((4, windows - 1)), dma((4, windows - 1)),
            dma((4, blocks - 1)), dma((4, blocks - 1)),
            dma((4, blocks)), dma((4, blocks)),
        ],
        compiler_params=pltpu.CompilerParams(
            collective_id=0, has_side_effects=True, vmem_limit_bytes=48 * 1024 * 1024
        ),
        cost_estimate=pl.CostEstimate(flops=5 * 10**9, bytes_accessed=4 * 10**6, transcendentals=0),
    )(white, tile_list, weights, cosines, sines)


def solution(mesh):
    placed = (P("win", "tile", None), P("tile", None), P("tile", None, None))
    return jax.shard_map(
        shards, mesh=mesh, in_specs=placed, out_specs=P("tile", "win", None), check_vma=False
    )
```

```python
import functools
import math

import jax
import jax.numpy as jnp
import ml_dtypes
import numpy as np
from jax import lax
from jax.experimental import pallas as pl
from jax.experimental.pallas import tpu as pltpu
from jax.sharding import PartitionSpec as P

CB = 256
NT = 8192
F = 2048
F_LO = 64
LAGS = 4
LAG_STEP = 25


BINS = 256
PIECES = 2
ORDER = np.argsort((F_LO + np.arange(F)) % 4, kind="stable")
FREQS = F_LO + ORDER


def quarter_table():
    phase = (np.arange(NT // 4)[:, None] * FREQS[None, :]) % NT
    angle = (phase * (2.0 * math.pi / NT)).reshape(NT // 4, F // BINS, 1, BINS)
    both = np.concatenate([np.cos(angle), np.sin(angle)], axis=2)
    return both.transpose(1, 0, 2, 3).reshape(F // BINS, NT // 4, 2 * BINS).astype(ml_dtypes.bfloat16)


def lag_tables():
    lags = (np.arange(LAGS) - LAGS // 2) * LAG_STEP
    phase = ((lags[:, None] * FREQS[None, :]) % NT) * (2.0 * math.pi / NT)
    return np.cos(phase).astype(np.float32), np.sin(phase).astype(np.float32)


def transform_kernel(signal, window, table, white, tapered, spectrum, power_sum):
    rows = signal.shape[1]
    quarter = NT // 4
    step = pl.program_id(0)

    @pl.when(step == 0)
    def _():
        total = jnp.zeros((rows, 1), jnp.float32)
        for part in range(4):
            values = signal[0, :, part * quarter : (part + 1) * quarter].astype(jnp.float32)
            total = total + jnp.sum(values, axis=-1, keepdims=True)
        mean = total / NT
        for part in range(4):
            cols = pl.ds(part * quarter, quarter)
            values = (signal[0, :, cols].astype(jnp.float32) - mean) * window[:, cols]
            tapered[pl.ds(part * rows, rows), :] = values.astype(jnp.bfloat16)
        power_sum[...] = jnp.zeros_like(power_sum)

    product = jnp.dot(tapered[...], table[0], preferred_element_type=jnp.float32)
    residue = step // (F // 4 // BINS)
    real_total = product[:rows, :BINS]
    imag_total = -product[:rows, BINS:]
    for part in range(1, 4):
        cos_part = product[part * rows : (part + 1) * rows, :BINS]
        sin_part = product[part * rows : (part + 1) * rows, BINS:]
        turn = (part * residue) % 4
        c = jnp.where(turn == 0, 1.0, jnp.where(turn == 2, -1.0, 0.0))
        d = jnp.where(turn == 1, -1.0, jnp.where(turn == 3, 1.0, 0.0))
        real_total = real_total + (c * cos_part + d * sin_part)
        imag_total = imag_total + (d * cos_part - c * sin_part)
    start = pl.multiple_of(step * BINS, BINS)
    spectrum[:, pl.ds(start, BINS)] = real_total
    spectrum[:, pl.ds(F + start, BINS)] = imag_total
    power = real_total * real_total + imag_total * imag_total
    power_sum[...] += jnp.sum(power, axis=-1, keepdims=True)

    @pl.when(step == F // BINS - 1)
    def _():
        floor = 0.01 * (power_sum[...] / F) + 1e-06
        for part in range(F // 512):
            real_cols = pl.ds(part * 512, 512)
            imag_cols = pl.ds(F + part * 512, 512)
            real_part = spectrum[:, real_cols]
            imag_part = spectrum[:, imag_cols]
            scale = lax.rsqrt(real_part * real_part + imag_part * imag_part + floor)
            white[:, real_cols] = (real_part * scale).astype(jnp.bfloat16)
            white[:, imag_cols] = (imag_part * scale).astype(jnp.bfloat16)


def transform(signal):
    rows = signal.shape[1]
    window = (0.5 - 0.5 * np.cos(np.arange(NT) * (2.0 * math.pi / NT))).astype(np.float32)[None]
    return pl.pallas_call(
        transform_kernel,
        grid=(F // BINS,),
        out_shape=jax.ShapeDtypeStruct((rows, 2 * F), jnp.bfloat16),
        in_specs=[
            pl.BlockSpec((1, rows, NT), lambda step: (0, 0, 0)),
            pl.BlockSpec((1, NT), lambda step: (0, 0)),
            pl.BlockSpec((1, NT // 4, 2 * BINS), lambda step: (step, 0, 0)),
        ],
        out_specs=pl.BlockSpec((rows, 2 * F), lambda step: (0, 0)),
        scratch_shapes=[
            pltpu.VMEM((4 * rows, NT // 4), jnp.bfloat16),
            pltpu.VMEM((rows, 2 * F), jnp.float32),
            pltpu.VMEM((rows, 1), jnp.float32),
        ],
        compiler_params=pltpu.CompilerParams(vmem_limit_bytes=56 * 1024 * 1024),
        cost_estimate=pl.CostEstimate(flops=9 * 10**9, bytes_accessed=20 * 10**6, transcendentals=0),
    )(signal, window, quarter_table())


def correlate_kernel(
    blocks, windows,
    white, pairs, weights, cosines, sines,
    out,
    left, left_next, right_near, right_far, rotated, product, outgoing, incoming, own_rows, gathered,
    half_send, half_recv, local_sem, win_send, win_recv, tile_send, tile_recv, pass_send, pass_recv,
):
    half = white.shape[0]
    rows_here = CB // windows
    tile = lax.axis_index("tile")
    win = lax.axis_index("win")
    chip, core = tile // 2, tile % 2
    sibling = chip * 2 + (1 - core)
    few = half // PIECES
    my_half = pl.ds(pl.multiple_of(core * half, half), half)

    def holds(which):
        even = which % 2 == 0
        far = which + 2 < blocks
        across = jnp.logical_and(which % 2 == 1, which >= 3)
        return [tile_here for tile_here in (which >= 0, even, far, across) for _ in range(PIECES)]

    mine = holds(chip)
    even, far, across = mine[PIECES], mine[2 * PIECES], mine[3 * PIECES]

    def remote(src, dst, send, recv, **where):
        return pltpu.make_async_remote_copy(
            src_ref=src, dst_ref=dst, send_sem=send, recv_sem=recv,
            device_id=where, device_id_type=pl.DeviceIdType.MESH,
        )

    def chip_ahead(step):
        return lax.rem(chip + step, blocks)

    barrier = pltpu.get_barrier_semaphore()
    pl.semaphore_signal(barrier, inc=1, device_id={"tile": sibling}, device_id_type=pl.DeviceIdType.MESH)
    for step in range(1, blocks):
        pl.semaphore_signal(
            barrier, inc=1, device_id={"tile": chip_ahead(step) * 2 + core}, device_id_type=pl.DeviceIdType.MESH
        )
    for step in range(1, windows):
        pl.semaphore_signal(
            barrier, inc=1, device_id={"win": lax.rem(win + step, windows)}, device_id_type=pl.DeviceIdType.MESH
        )
    pl.semaphore_wait(barrier, blocks + windows - 1)

    sends_near = chip >= 1
    sends_far = chip >= 2
    sends_left = jnp.logical_and(chip % 2 == 1, far)
    partner = lax.rem(chip + 1 - 2 * (chip % 2) + blocks, blocks) * 2 + core
    to_near, to_far = [], []
    for piece in range(PIECES):
        rows = pl.ds(piece * few, few)
        near_at, far_at = 3 + 2 * piece, 4 + 2 * piece
        to_near.append(
            remote(white.at[rows], right_near.at[rows], half_send.at[near_at], half_recv.at[near_at], tile=partner)
        )
        to_far.append(
            remote(
                white.at[rows], right_far.at[rows], half_send.at[far_at], half_recv.at[far_at],
                tile=chip_ahead(blocks - 2) * 2 + core,
            )
        )
    to_left = remote(
        white, left_next.at[my_half], half_send.at[0], half_recv.at[0], tile=chip_ahead(2) * 2 + core
    )
    to_sibling = remote(white, left.at[my_half], half_send.at[2], half_recv.at[2], tile=sibling)
    pass_on = remote(
        left_next.at[my_half], left_next.at[my_half], half_send.at[1], half_recv.at[1], tile=sibling
    )
    keep = pltpu.make_async_copy(white, left.at[my_half], local_sem)

    for piece in range(PIECES):
        pl.when(sends_near)(to_near[piece].start)
        pl.when(sends_far)(to_far[piece].start)
    pl.when(sends_left)(to_left.start)
    to_sibling.start()
    keep.start()

    def rotate(right, piece):
        chunk = 512
        rows = pl.ds(piece * few, few)
        for part in range(F // chunk):
            real_cols = pl.ds(part * chunk, chunk)
            imag_cols = pl.ds(F + part * chunk, chunk)
            real_part = right[rows, real_cols].astype(jnp.float32)
            imag_part = right[rows, imag_cols].astype(jnp.float32)
            for k in range(LAGS):
                c = cosines[pl.ds(k, 1), real_cols]
                s = sines[pl.ds(k, 1), real_cols]
                lag_rows = pl.ds(k * few, few)
                rotated[lag_rows, real_cols] = (real_part * c + imag_part * s).astype(jnp.bfloat16)
                rotated[lag_rows, imag_cols] = (imag_part * c - real_part * s).astype(jnp.bfloat16)

    def win_copy(t, step):
        peer = lax.rem(win + step, windows)
        rows = pl.ds(pl.multiple_of(peer * rows_here, rows_here), rows_here)
        return remote(
            outgoing.at[t, rows], incoming.at[t, step - 1],
            win_send.at[t, step - 1], win_recv.at[t, step - 1], win=peer,
        )

    def spread(index):
        return 1.0 + index.astype(jnp.float32) / windows

    def multiply(t, rows_ref):
        product[...] = lax.dot_general(
            rows_ref[...], rotated[...], (((1,), (1,)), ((), ())), preferred_element_type=jnp.float32
        )
        outgoing[t] = (product[...] * spread(win)).astype(jnp.bfloat16)
        own_rows[t] = product[pl.ds(pl.multiple_of(win * rows_here, rows_here), rows_here), :]
        for step in range(1, windows):
            win_copy(t, step).start()

    def tile_copy(t, step):
        spot = gathered.at[core, chip, t]
        return remote(
            spot, spot, tile_send.at[t, step - 1], tile_recv.at[t, step - 1], tile=chip_ahead(step) * 2 + core
        )

    def pass_copy(t, step):
        spot = gathered.at[core, chip_ahead(blocks - step), t]
        return remote(spot, spot, pass_send.at[t, step], pass_recv.at[t, step], tile=sibling)

    def collect(t):
        total = own_rows[t]
        for step in range(1, windows):
            win_copy(t, step).wait_recv()
            sender = lax.rem(win + windows - step, windows)
            total = total + incoming[t, step - 1].astype(jnp.float32) / spread(sender)
        gathered[core, chip, t] = total
        for step in range(1, blocks):
            tile_copy(t, step).start()
        pass_copy(t, 0).start()

    keep.wait()
    for piece in range(PIECES):
        rotate(white, piece)
        if piece == 0:
            to_sibling.wait_recv()
        multiply(piece, left)

    for piece in range(PIECES):

        @pl.when(even)
        def _():
            to_near[piece].wait_recv()
            rotate(right_near, piece)
            multiply(PIECES + piece, left)

        @pl.when(far)
        def _():
            to_far[piece].wait_recv()
            rotate(right_far, piece)
            multiply(2 * PIECES + piece, left)

        @pl.when(across)
        def _():
            if piece == 0:
                to_left.wait_recv()
                pass_on.start()
            to_near[piece].wait_recv()
            rotate(right_near, piece)
            if piece == 0:
                pass_on.wait_recv()
            multiply(3 * PIECES + piece, left_next)

        if piece == 0:
            for t in range(PIECES):
                collect(t)

    for t in [tile_kind * PIECES + piece for piece in range(PIECES) for tile_kind in range(1, 4)]:
        pl.when(mine[t])(functools.partial(collect, t))

    for t in [tile_kind * PIECES + piece for piece in range(PIECES) for tile_kind in range(4)]:
        for step in range(1, blocks):

            @pl.when(holds(chip_ahead(blocks - step))[t])
            def _():
                tile_copy(t, step).wait_recv()
                pass_copy(t, step).start()

    for t in [tile_kind * PIECES + piece for piece in range(PIECES) for tile_kind in range(4)]:
        for step in range(blocks):

            @pl.when(holds(chip_ahead(blocks - step))[t])
            def _():
                pass_copy(t, step).wait_recv()

    for slot in range(out.shape[0]):
        row_block = pairs[slot, 0]
        distance = pairs[slot, 1] - row_block
        live = row_block >= 0
        row_block = jnp.maximum(row_block, 0)
        step_in = jnp.logical_and(distance == 1, row_block % 2 == 1)
        place = jnp.where(step_in, row_block + 2, row_block)
        which = jnp.where(step_in, 3, distance)
        for side in range(2):
            values = [gathered[side, place, which * PIECES + piece] for piece in range(PIECES)]
            side_cols = pl.ds(side * half, half)
            factor = weights[slot, :, side_cols]
            for k in range(LAGS):
                lag = jnp.concatenate([value[:, k * few : (k + 1) * few] for value in values], axis=1)
                out[slot, :, pl.ds(k * CB + side * half, half)] = jnp.where(live, lag * factor, 0.0)

    for piece in range(PIECES):
        pl.when(sends_near)(to_near[piece].wait_send)
        pl.when(sends_far)(to_far[piece].wait_send)
    pl.when(sends_left)(to_left.wait_send)
    to_sibling.wait_send()
    pl.when(across)(pass_on.wait_send)

    for t in [tile_kind * PIECES + piece for piece in range(PIECES) for tile_kind in range(4)]:

        @pl.when(mine[t])
        def _():
            for step in range(1, windows):
                win_copy(t, step).wait_send()
            for step in range(1, blocks):
                tile_copy(t, step).wait_send()

        for step in range(blocks):
            pl.when(holds(chip_ahead(blocks - step))[t])(pass_copy(t, step).wait_send)


def shards(signal, tile_list, band_mask):
    white = transform(signal)
    slot_count = tile_list.shape[0]
    windows = lax.axis_size("win")
    half = white.shape[0]
    blocks = lax.axis_size("tile") * half // CB
    rows_here = CB // windows
    norm = 1.0 / math.sqrt(F * windows)
    first_row = lax.axis_index("win") * rows_here
    mask_rows = lax.dynamic_slice_in_dim(band_mask, first_row, rows_here, 1)
    weights = mask_rows.astype(jnp.float32) * norm
    cosines, sines = lag_tables()
    vmem = pl.BlockSpec(memory_space=pltpu.VMEM)
    dma = pltpu.SemaphoreType.DMA
    width = LAGS * half // PIECES
    units = 4 * PIECES
    return pl.pallas_call(
        functools.partial(correlate_kernel, blocks, windows),
        out_shape=jax.ShapeDtypeStruct((slot_count, rows_here, LAGS * CB), jnp.float32),
        in_specs=[vmem, pl.BlockSpec(memory_space=pltpu.SMEM), vmem, vmem, vmem],
        out_specs=vmem,
        scratch_shapes=[
            pltpu.VMEM((CB, 2 * F), jnp.bfloat16),
            pltpu.VMEM((CB, 2 * F), jnp.bfloat16),
            pltpu.VMEM((half, 2 * F), jnp.bfloat16),
            pltpu.VMEM((half, 2 * F), jnp.bfloat16),
            pltpu.VMEM((width, 2 * F), jnp.bfloat16),
            pltpu.VMEM((CB, width), jnp.float32),
            pltpu.VMEM((units, CB, width), jnp.bfloat16),
            pltpu.VMEM((units, windows - 1, rows_here, width), jnp.bfloat16),
            pltpu.VMEM((units, rows_here, width), jnp.float32),
            pltpu.VMEM((2, blocks, units, rows_here, width), jnp.float32),
            dma((3 + 2 * PIECES,)), dma((3 + 2 * PIECES,)), dma,
            dma((units, windows - 1)), dma((units, windows - 1)),
            dma((units, blocks - 1)), dma((units, blocks - 1)),
            dma((units, blocks)), dma((units, blocks)),
        ],
        compiler_params=pltpu.CompilerParams(
            collective_id=0, has_side_effects=True, vmem_limit_bytes=48 * 1024 * 1024
        ),
        cost_estimate=pl.CostEstimate(flops=5 * 10**9, bytes_accessed=4 * 10**6, transcendentals=0),
    )(white, tile_list, weights, cosines, sines)


def solution(mesh):
    placed = (P("win", "tile", None), P("tile", None), P("tile", None, None))
    return jax.shard_map(
        shards, mesh=mesh, in_specs=placed, out_specs=P("tile", "win", None), check_vma=False
    )
```
